32 devices in a mesh: head: 4 (over y, x), blk: 4 (over z), dp: 2 (over core).
Axes of the slice: x: 2, y: 2, z: 4, core: 2. Of those that a mesh axis runs over, the one named last changes fastest.
Arguments:
- layer_input: bfloat16 [4096, 4096], P(('dp', 'blk', 'head')), may hold values from -6 to 6
- rot_queries: bfloat16 [4096, 4096], P(('dp', 'blk', 'head')), may hold values from -6 to 6
- rot_keys: bfloat16 [4096, 512], P(('dp', 'blk', 'head')), may hold values from -6 to 6
- value_rows: bfloat16 [4096, 512], P(('dp', 'blk', 'head')), may hold values from -6 to 6
- attn_output: bfloat16 [4096, 4096], P(('dp', 'blk', 'head')), may hold values from -3 to 3
- output_grad: bfloat16 [4096, 4096], P(('dp', 'blk', 'head')), may hold values from -1.5 to 1.5
- log_norm: float32 [4096, 32], P(('dp', 'blk'), 'head'), may hold values from 6 to 8
- lengths: int32 [2, 3], P('dp'), may hold values from 128 to 1280, as said below
Outputs:
- dw_query: float32 [4096, 4096], P(('blk', 'dp'), 'head')
- dw_key: float32 [4096, 512], P(('blk', 'dp'), 'head')
- dw_value: float32 [4096, 512], P(('blk', 'dp'), 'head')
The draws below stay inside these ranges and needn't reach their ends.
Inputs may be any that keep to these rules, and one draw needn't show every extreme that they name: `lengths`: each row sums to 2048; every length is a multiple of 128; in every row one document has length 1280.
All inputs are finite; a program needn't handle non-finite values.
Results may differ from the reference program's by a relative error of at most 0.0041.
Values may be sent and summed in bfloat16 or wider, within the bound.
A program may use at most 128 MiB of HBM per device.

```python
import math
import jax
import jax.numpy as jnp
from jax import lax

DW = 4096
HQ = 32
HK = 4
HD = 128
UNIT = 128
GQ = 8
TOK_GRP = 2048
TOKENS = 4096
MOST_LEN = 1280
N_DP = 2


def draw_lengths(key, part):
    key = jax.random.fold_in(key, 11)
    units = TOK_GRP // UNIT
    longest = MOST_LEN // UNIT
    spare = units - longest
    key_first, key_order = jax.random.split(key)
    first = jax.random.randint(key_first, (N_DP,), 1, spare, dtype=jnp.int32)
    table = jnp.stack([jnp.full((N_DP,), longest, jnp.int32), first, spare - first], axis=1)
    order = jax.vmap(lambda k: jax.random.permutation(k, 3))(jax.random.split(key_order, N_DP))
    return (jnp.take_along_axis(table, order.astype(jnp.int32), axis=1) * UNIT).astype(jnp.int32)


def level_of(own_key, extent, pieces, smallest, largest):
    gain = 1.0
    for axis_at, blocks in pieces:
        steps = jax.random.uniform(jax.random.fold_in(jax.random.fold_in(own_key, 6), axis_at), (blocks,), jnp.float32, smallest / len(pieces), largest / len(pieces))
        gain = gain * jnp.repeat(jnp.exp(steps), extent[axis_at] // blocks).reshape((-1,) + (1,) * (len(extent) - 1 - axis_at))
    return gain


def bell_draw(key, shape, width, reach, pieces=(), kind=jnp.bfloat16):
    result = jax.random.normal(key, shape, jnp.float32) * width
    if len(pieces) > 0:
        result = level_of(key, shape, pieces, -0.22, 0.18) * result
    return jnp.clip(result, min=-reach, max=reach).astype(kind)


def setup_inputs(seed: int = 0) -> dict:
    key_of = jax.random.split(jax.random.key(seed), 9)
    return {
        "layer_input": bell_draw(key_of[0], (TOKENS, DW), 1.0, 6.0, ((0, 32),)),
        "rot_queries": bell_draw(key_of[1], (TOKENS, HQ * HD), 1.0, 6.0, ((0, 32),)),
        "rot_keys": bell_draw(key_of[2], (TOKENS, HK * HD), 1.0, 6.0, ((0, 32),)),
        "value_rows": bell_draw(key_of[3], (TOKENS, HK * HD), 1.0, 6.0, ((0, 32),)),
        "attn_output": bell_draw(key_of[4], (TOKENS, HQ * HD), 0.2, 3.0, ((0, 32),)),
        "output_grad": bell_draw(key_of[5], (TOKENS, HQ * HD), 0.1, 1.5, ((0, 32),)),
        "log_norm": jnp.clip(6.0 + 2.0 * jax.random.uniform(key_of[6], (TOKENS, HQ), jnp.float32) ** level_of(key_of[6], (TOKENS, HQ), ((0, 8), (1, 4)), -0.2, 0.2), 6.0, 8.0),
        "lengths": draw_lengths(jax.random.fold_in(key_of[8], 71), 0),
    }


def doc_place(ends, lengths_row, index):
    after = (index[:, None] >= ends[None, :]).astype(jnp.int32)
    doc = jnp.sum(after, axis=1).astype(jnp.int32)
    first = jnp.sum(after * lengths_row[None, :], axis=1).astype(jnp.int32)
    return doc, index - first


def undo_rotary(grad, position):
    half = grad.shape[2] // 2
    steps_j = jnp.arange(half).astype(jnp.float32)
    inverse = jnp.exp(-math.log(500000.0) * 2.0 * steps_j / grad.shape[2])
    angle = position.astype(jnp.float32)[:, None] * inverse[None, :]
    cosine = jnp.cos(angle)[:, None, :]
    sine = jnp.sin(angle)[:, None, :]
    first = grad[:, :, :half]
    second = grad[:, :, half:]
    return jnp.concatenate([first * cosine + second * sine, second * cosine - first * sine], axis=2)


def lowered(value):
    return lax.optimization_barrier(value.astype(jnp.bfloat16)).astype(jnp.float32)


def reference(layer_input, rot_queries, rot_keys, value_rows, attn_output, output_grad, log_norm, lengths):
    scale = HD ** -0.5

    def one_group(total, group):
        inputs, queries, keys_in, values_in, outputs, grads_out, norms, lengths_row = group
        count = queries.shape[0]
        index = jnp.arange(count, dtype=jnp.int32)
        ends = jnp.cumsum(lengths_row).astype(jnp.int32)
        doc, position = doc_place(ends, lengths_row, index)
        allowed = (doc[:, None] == doc[None, :]) & (index[None, :] <= index[:, None])
        grad_full = grads_out.astype(jnp.float32).reshape(count, HK, GQ, HD)
        delta = jnp.sum(grad_full * outputs.astype(jnp.float32).reshape(count, HK, GQ, HD), axis=3)
        query_f = queries.astype(jnp.float32).reshape(count, HK, GQ, HD).transpose(1, 0, 2, 3)
        grad_f = grad_full.transpose(1, 0, 2, 3)
        key_f = keys_in.astype(jnp.float32).reshape(count, HK, HD).transpose(1, 0, 2)
        value_f = values_in.astype(jnp.float32).reshape(count, HK, HD).transpose(1, 0, 2)
        norm_f = norms.reshape(count, HK, GQ).transpose(1, 0, 2)
        delta_f = delta.transpose(1, 0, 2)

        def one_head(items):
            query_h, grad_h, key_h, value_h, norm_h, delta_h = items
            score = jnp.einsum('tgd,sd->gts', query_h, key_h) * scale
            prob = jnp.where(allowed[None], jnp.exp(score - norm_h.T[:, :, None]), 0.0)
            dprob = jnp.einsum('tgd,sd->gts', grad_h, value_h)
            dscore = prob * (dprob - delta_h.T[:, :, None])
            prob_low = lowered(prob)
            dscore_low = lowered(dscore)
            grad_q = jnp.einsum('gts,sd->tgd', dscore_low, key_h) * scale
            grad_k = jnp.einsum('gts,tgd->sd', dscore_low, query_h) * scale
            grad_v = jnp.einsum('gts,tgd->sd', prob_low, grad_h)
            return grad_q, grad_k, grad_v

        grad_q, grad_k, grad_v = lax.map(one_head, (query_f, grad_f, key_f, value_f, norm_f, delta_f))
        grad_q = grad_q.transpose(1, 0, 2, 3).reshape(count, HQ, HD)
        grad_k = grad_k.transpose(1, 0, 2)
        grad_v = grad_v.transpose(1, 0, 2).reshape(count, HK * HD)
        dq_low = undo_rotary(grad_q, position).reshape(count, HQ * HD).astype(jnp.bfloat16)
        dk_low = undo_rotary(grad_k, position).reshape(count, HK * HD).astype(jnp.bfloat16)
        dv_low = grad_v.astype(jnp.bfloat16)
        parts = (jnp.dot(inputs.T, dq_low, preferred_element_type=jnp.float32),
                 jnp.dot(inputs.T, dk_low, preferred_element_type=jnp.float32),
                 jnp.dot(inputs.T, dv_low, preferred_element_type=jnp.float32))
        return (total[0] + parts[0], total[1] + parts[1], total[2] + parts[2]), None

    arrays = (layer_input, rot_queries, rot_keys, value_rows, attn_output, output_grad, log_norm)
    groups = tuple(a.reshape(N_DP, TOK_GRP, a.shape[1]) for a in arrays) + (lengths,)
    start_sum = (jnp.zeros((DW, HQ * HD), jnp.float32), jnp.zeros((DW, HK * HD), jnp.float32),
                 jnp.zeros((DW, HK * HD), jnp.float32))
    total, _ = lax.scan(one_group, start_sum, groups)
    return total[0], total[1], total[2]
```

```python
import functools
import math

import jax
import jax.numpy as jnp
from jax import lax
from jax.experimental import pallas as pl
from jax.experimental.pallas import tpu as pltpu
from jax.sharding import PartitionSpec as P

HQ = 32
HD = 128
GQ = 8
UNIT = 128
MOST_LEN = 1280
BACK = MOST_LEN - UNIT
TILE = 256
LOG2E = math.log2(math.e)
SCALE = HD ** (-0.5)


def contract_rows(left, right):
    return lax.dot_general(
        left, right, (((0,), (0,)), ((), ())), preferred_element_type=jnp.float32
    )


def contract_cols(left, right):
    return lax.dot_general(
        left, right, (((1,), (1,)), ((), ())), preferred_element_type=jnp.float32
    )


def doc_place(ends, lengths_row, index):
    after = (index[:, None] >= ends[None, :]).astype(jnp.int32)
    first = jnp.sum(after * lengths_row[None, :], axis=1)
    return (first, index - first)


def attention_kernel(
    chunk, q_ref, g_ref, k_ref, v_ref, kt_ref, norm_ref, delta_ref, start_ref, cos_ref, sin_ref,
    dk_in_ref, dv_in_ref, dq_ref, dk_ref, dv_ref, bias_ref
):
    rows = q_ref.shape[0]
    tiles = rows // TILE
    span = TILE + BACK

    @pl.when(pl.program_id(0) == 0)
    def _():
        dk_ref[...] = dk_in_ref[...]
        dv_ref[...] = dv_in_ref[...]
        for j in range(tiles):
            key_at = lax.broadcasted_iota(jnp.int32, (span, TILE), 0) + j * TILE
            query_at = lax.broadcasted_iota(jnp.int32, (span, TILE), 1) + (j * TILE + BACK)
            first = start_ref[:, j * TILE : (j + 1) * TILE]
            allowed = (key_at >= first) & (key_at <= query_at)
            bias_ref[j] = jnp.where(allowed, 0.0, -1e30)

    for j in range(tiles):
        here = slice(j * TILE, (j + 1) * TILE)
        query = q_ref[here, :]
        grad = g_ref[here, :]
        norm = norm_ref[0, :, here]
        delta = delta_ref[0, :, here]
        dq_t = jnp.zeros((HD, TILE), jnp.float32)
        for c in range(0, span, chunk):
            keys = slice(j * TILE + c, j * TILE + c + chunk)
            score = contract_cols(k_ref[keys, :], query)
            prob = jnp.exp2((score * (SCALE * LOG2E) - norm) + bias_ref[j, c : c + chunk, :])
            dprob = contract_cols(v_ref[keys, :], grad)
            dscore = (prob * (dprob - delta)).astype(jnp.bfloat16)
            dv_ref[keys, :] += jnp.dot(
                prob.astype(jnp.bfloat16), grad, preferred_element_type=jnp.float32
            )
            dk_ref[keys, :] += jnp.dot(dscore, query, preferred_element_type=jnp.float32)
            dq_t += jnp.dot(kt_ref[:, keys], dscore, preferred_element_type=jnp.float32)
        cosine = cos_ref[:, here]
        sine = sin_ref[:, here]
        upper = dq_t[: HD // 2]
        lower = dq_t[HD // 2 :]
        turned = jnp.concatenate(
            [upper * cosine + lower * sine, lower * cosine - upper * sine], axis=0
        )
        dq_ref[here, :] = turned.T.astype(jnp.bfloat16)


def attention(first_head, heads, chunk, queries, grads, keys, values, keys_t, norm, delta, start,
              cosine, sine, dk_in, dv_in):
    rows = queries.shape[0]
    window = keys.shape[0]
    whole = lambda shape: pl.BlockSpec(shape, lambda h: (0,) * len(shape))
    per_head = pl.BlockSpec((rows, HD), lambda h: (0, h + first_head))
    per_row = pl.BlockSpec((1, 1, rows), lambda h: (h + first_head, 0, 0))
    work = heads * (rows // TILE) * (TILE + BACK) * TILE
    return pl.pallas_call(
        functools.partial(attention_kernel, chunk),
        grid=(heads,),
        in_specs=[
            per_head, per_head, whole((window, HD)), whole((window, HD)), whole((HD, window)),
            per_row, per_row, whole((1, rows)), whole((HD // 2, rows)), whole((HD // 2, rows)),
            whole((window, HD)), whole((window, HD)),
        ],
        out_specs=[
            pl.BlockSpec((rows, HD), lambda h: (0, h)), whole((window, HD)), whole((window, HD)),
        ],
        out_shape=[
            jax.ShapeDtypeStruct((rows, heads * HD), jnp.bfloat16),
            jax.ShapeDtypeStruct((window, HD), jnp.float32),
            jax.ShapeDtypeStruct((window, HD), jnp.float32),
        ],
        scratch_shapes=[pltpu.VMEM((rows // TILE, TILE + BACK, TILE), jnp.float32)],
        compiler_params=pltpu.CompilerParams(vmem_limit_bytes=40 * 1024 * 1024),
        cost_estimate=pl.CostEstimate(
            flops=work * HD * 10, bytes_accessed=4 * rows * heads * HD, transcendentals=work
        ),
    )(queries, grads, keys, values, keys_t, norm, delta, start, cosine, sine, dk_in, dv_in)


def undo_rotary(grad, cosine, sine):
    half = grad.shape[1] // 2
    first = grad[:, :half]
    second = grad[:, half:]
    return jnp.concatenate([first * cosine + second * sine, second * cosine - first * sine], axis=1)


def window_parts(row_count):
    parts = []
    shift = 1
    left = BACK
    while left > 0:
        count = min(left, row_count)
        parts.append((shift, row_count - count, count))
        left -= count
        shift += 1
    return parts


def swap_heads(array):
    return lax.all_to_all(array, "head", split_axis=1, concat_axis=0, tiled=True)


def on_device(
    layer_input, rot_queries, rot_keys, value_rows, attn_output, output_grad, log_norm, lengths
):
    head_count = log_norm.shape[1]
    head_devices = lax.axis_size("head")
    blocks = lax.axis_size("blk")
    local_count = rot_queries.shape[0]
    row_count = local_count * head_devices
    own_delta = jnp.sum(
        (output_grad.astype(jnp.float32) * attn_output.astype(jnp.float32)).reshape(
            local_count, HQ, HD
        ),
        axis=2,
    )
    high = lax.reduce_precision(own_delta, 8, 7)
    middle = lax.reduce_precision(own_delta - high, 8, 7)
    low = own_delta - high - middle
    by_head = lambda array: array.astype(jnp.bfloat16).reshape(local_count, head_devices, -1)
    packed = jnp.concatenate(
        [
            by_head(rot_keys), by_head(value_rows), by_head(high), by_head(middle), by_head(low),
            jnp.zeros((local_count, head_devices, HD - 3 * head_count), jnp.bfloat16),
        ],
        axis=2,
    ).reshape(local_count, -1)
    packed = swap_heads(packed)
    pairs = packed[:, : 2 * HD]
    terms = packed[:, 2 * HD :].astype(jnp.float32)
    delta = (
        terms[:, :head_count]
        + terms[:, head_count : 2 * head_count]
        + terms[:, 2 * head_count : 3 * head_count]
    )
    parts = window_parts(row_count)
    pieces = [pairs]
    for shift, first, count in parts:
        part = pairs[first : first + count]
        if shift < blocks:
            part = lax.ppermute(part, "blk", [(b, b + shift) for b in range(blocks - shift)])
        else:
            part = jnp.zeros_like(part)
        pieces.insert(0, part)
    queries = swap_heads(rot_queries)
    grads_out = swap_heads(output_grad)
    inputs = lax.all_to_all(layer_input, ("blk", "dp"), split_axis=1, concat_axis=0, tiled=True)
    groups = lax.axis_size("blk") * lax.axis_size("dp")
    inputs = lax.all_gather(inputs.reshape(groups, local_count, -1), "head", axis=1, tiled=True)
    inputs = inputs.reshape(groups * row_count, -1)
    keys_values = jnp.concatenate(pieces, axis=0)
    keys = keys_values[:, :HD]
    values = keys_values[:, HD:]

    lengths_row = lengths[0]
    ends = jnp.cumsum(lengths_row)
    first_row = lax.axis_index("blk") * row_count
    first, position = doc_place(
        ends, lengths_row, first_row + jnp.arange(row_count, dtype=jnp.int32)
    )
    start = (first - first_row + BACK)[None, :]
    steps_j = jnp.arange(HD // 2).astype(jnp.float32)
    inverse = jnp.exp(-math.log(500000.0) * 2.0 * steps_j / HD)
    angle = position.astype(jnp.float32)[:, None] * inverse[None, :]
    cosine = jnp.cos(angle) * SCALE
    sine = jnp.sin(angle) * SCALE

    zero = jnp.zeros((keys.shape[0], HD), jnp.float32)
    shared = (
        queries, grads_out, keys, values, keys.T, (log_norm.T * LOG2E)[:, None, :],
        delta.T[:, None, :], start, cosine.T, sine.T,
    )
    half = head_count // 2
    dq_first, dk_part, dv_part = attention(0, half, 704, *shared, zero, zero)
    all_first = lax.all_gather(dq_first, ("blk", "dp"), axis=0, tiled=True)
    dq_second, dk_part, dv_part = attention(half, half, 704, *shared, dk_part, dv_part)
    all_second = lax.all_gather(dq_second, ("blk", "dp"), axis=0, tiled=True)

    key_sums = jnp.concatenate([dk_part, dv_part], axis=1)
    total = key_sums[BACK:]
    at = BACK
    for shift, first, count in parts:
        at -= count
        if shift < blocks:
            got = lax.ppermute(
                key_sums[at : at + count].astype(jnp.bfloat16),
                "blk",
                [(b + shift, b) for b in range(blocks - shift)],
            ).astype(jnp.float32)
            total = total + jnp.pad(got, ((first, 0), (0, 0)))
    key_grads = jnp.concatenate(
        [undo_rotary(total[:, :HD], cosine, sine), total[:, HD:]], axis=1
    ).astype(jnp.bfloat16)
    all_keys = lax.all_gather(key_grads, ("blk", "dp"), axis=0, tiled=True)

    dw_first = contract_rows(inputs, all_first)
    dw_second = contract_rows(inputs, all_second)
    dw_keys = contract_rows(inputs, all_keys)
    return (
        jnp.concatenate([dw_first, dw_second], axis=1),
        dw_keys[:, :HD],
        dw_keys[:, HD:],
    )


def solution(mesh):
    placed = (
        P(("dp", "blk", "head"), None),
        P(("dp", "blk", "head"), None),
        P(("dp", "blk", "head"), None),
        P(("dp", "blk", "head"), None),
        P(("dp", "blk", "head"), None),
        P(("dp", "blk", "head"), None),
        P(("dp", "blk"), "head"),
        P("dp", None),
    )
    return jax.shard_map(
        on_device,
        mesh=mesh,
        in_specs=placed,
        out_specs=(P(("blk", "dp"), "head"), P(("blk", "dp"), "head"), P(("blk", "dp"), "head")),
        check_vma=False,
    )
```

```python
import functools
import math

import jax
import jax.numpy as jnp
from jax import lax
from jax.experimental import pallas as pl
from jax.experimental.pallas import tpu as pltpu
from jax.sharding import PartitionSpec as P

HQ = 32
HD = 128
GQ = 8
UNIT = 128
MOST_LEN = 1280
BACK = MOST_LEN - UNIT
TILE = 256
LOG2E = math.log2(math.e)
SCALE = HD ** (-0.5)


def contract_rows(left, right):
    return lax.dot_general(
        left, right, (((0,), (0,)), ((), ())), preferred_element_type=jnp.float32
    )


def contract_cols(left, right):
    return lax.dot_general(
        left, right, (((1,), (1,)), ((), ())), preferred_element_type=jnp.float32
    )


def doc_place(ends, lengths_row, index):
    after = (index[:, None] >= ends[None, :]).astype(jnp.int32)
    first = jnp.sum(after * lengths_row[None, :], axis=1)
    return (first, index - first)


def attention_kernel(
    chunk, q_ref, g_ref, k_ref, v_ref, kt_ref, norm_ref, delta_ref, start_ref, cos_ref, sin_ref,
    dk_in_ref, dv_in_ref, dq_ref, dk_ref, dv_ref, bias_ref
):
    rows = q_ref.shape[0]
    tiles = rows // TILE
    span = TILE + BACK

    @pl.when(pl.program_id(0) == 0)
    def _():
        dk_ref[...] = dk_in_ref[...]
        dv_ref[...] = dv_in_ref[...]
        for j in range(tiles):
            key_at = lax.broadcasted_iota(jnp.int32, (span, TILE), 0) + j * TILE
            query_at = lax.broadcasted_iota(jnp.int32, (span, TILE), 1) + (j * TILE + BACK)
            first = start_ref[:, j * TILE : (j + 1) * TILE]
            allowed = (key_at >= first) & (key_at <= query_at)
            bias_ref[j] = jnp.where(allowed, 0.0, -1e30)

    for j in range(tiles):
        here = slice(j * TILE, (j + 1) * TILE)
        query = q_ref[here, :]
        grad = g_ref[here, :]
        norm = norm_ref[0, :, here]
        delta = delta_ref[0, :, here]
        dq_t = jnp.zeros((HD, TILE), jnp.float32)
        for c in range(0, span, chunk):
            keys = slice(j * TILE + c, j * TILE + c + chunk)
            score = contract_cols(k_ref[keys, :], query)
            prob = jnp.exp2((score * (SCALE * LOG2E) - norm) + bias_ref[j, c : c + chunk, :])
            dprob = contract_cols(v_ref[keys, :], grad)
            dscore = (prob * (dprob - delta)).astype(jnp.bfloat16)
            dv_ref[keys, :] += jnp.dot(
                prob.astype(jnp.bfloat16), grad, preferred_element_type=jnp.float32
            )
            dk_ref[keys, :] += jnp.dot(dscore, query, preferred_element_type=jnp.float32)
            dq_t += jnp.dot(kt_ref[:, keys], dscore, preferred_element_type=jnp.float32)
        cosine = cos_ref[:, here]
        sine = sin_ref[:, here]
        upper = dq_t[: HD // 2]
        lower = dq_t[HD // 2 :]
        turned = jnp.concatenate(
            [upper * cosine + lower * sine, lower * cosine - upper * sine], axis=0
        )
        dq_ref[here, :] = turned.T.astype(jnp.bfloat16)


def attention(first_head, heads, chunk, queries, grads, keys, values, keys_t, norm, delta, start,
              cosine, sine, dk_in, dv_in):
    rows = queries.shape[0]
    window = keys.shape[0]
    whole = lambda shape: pl.BlockSpec(shape, lambda h: (0,) * len(shape))
    per_head = pl.BlockSpec((rows, HD), lambda h: (0, h + first_head))
    per_row = pl.BlockSpec((1, 1, rows), lambda h: (h + first_head, 0, 0))
    work = heads * (rows // TILE) * (TILE + BACK) * TILE
    return pl.pallas_call(
        functools.partial(attention_kernel, chunk),
        grid=(heads,),
        in_specs=[
            per_head, per_head, whole((window, HD)), whole((window, HD)), whole((HD, window)),
            per_row, per_row, whole((1, rows)), whole((HD // 2, rows)), whole((HD // 2, rows)),
            whole((window, HD)), whole((window, HD)),
        ],
        out_specs=[
            pl.BlockSpec((rows, HD), lambda h: (0, h)), whole((window, HD)), whole((window, HD)),
        ],
        out_shape=[
            jax.ShapeDtypeStruct((rows, heads * HD), jnp.bfloat16),
            jax.ShapeDtypeStruct((window, HD), jnp.float32),
            jax.ShapeDtypeStruct((window, HD), jnp.float32),
        ],
        scratch_shapes=[pltpu.VMEM((rows // TILE, TILE + BACK, TILE), jnp.float32)],
        compiler_params=pltpu.CompilerParams(vmem_limit_bytes=40 * 1024 * 1024),
        cost_estimate=pl.CostEstimate(
            flops=work * HD * 10, bytes_accessed=4 * rows * heads * HD, transcendentals=work
        ),
    )(queries, grads, keys, values, keys_t, norm, delta, start, cosine, sine, dk_in, dv_in)


MESH = pl.DeviceIdType.MESH


def greet(peers):
    barrier = pltpu.get_barrier_semaphore()
    for peer in peers:
        pl.semaphore_signal(barrier, inc=1, device_id=peer, device_id_type=MESH)
    pl.semaphore_wait(barrier, len(peers))


def ring_peers(axis, size):
    here = lax.axis_index(axis)
    return [{axis: lax.rem(here + step, size)} for step in range(1, size)]


def group_peers(blocks, pairs):
    block = lax.axis_index("blk")
    side = lax.axis_index("dp")
    peers = []
    for step in range(1, blocks * pairs):
        peers.append(
            {
                "blk": lax.rem(block + step // pairs, blocks),
                "dp": lax.rem(side + step % pairs, pairs),
            }
        )
    return peers


def exchange_kernel(
    sizes, parts, q_ref, g_ref, k_ref, v_ref, d_ref, x_ref,
    qo_ref, go_ref, ko_ref, vo_ref, do_ref, xo_ref,
    head_send, head_recv, own_sem, shift_send, shift_recv, group_send, group_recv,
):
    head_devices, blocks, pairs = sizes
    me = lax.axis_index("head")
    block = lax.axis_index("blk")
    side = lax.axis_index("dp")
    count = q_ref.shape[0]
    head_list = ring_peers("head", head_devices)
    group_list = group_peers(blocks, pairs)
    greet(head_list + group_list)

    def source(index, owner):
        if index == 0:
            return k_ref.at[:, pl.ds(pl.multiple_of(owner * HD, HD), HD)]
        if index == 1:
            return v_ref.at[:, pl.ds(pl.multiple_of(owner * HD, HD), HD)]
        if index == 2:
            rows = d_ref.shape[0] // head_devices
            return d_ref.at[pl.ds(pl.multiple_of(owner * rows, 8), rows), :]
        wide = q_ref.shape[1] // head_devices
        columns = pl.ds(pl.multiple_of(owner * wide, HD), wide)
        return (q_ref if index == 3 else g_ref).at[:, columns]

    def target(index):
        if index <= 1:
            rows = pl.ds(pl.multiple_of(BACK + me * count, UNIT), count)
            return (ko_ref if index == 0 else vo_ref).at[rows, :]
        if index == 2:
            return do_ref.at[:, pl.ds(pl.multiple_of(me * count, UNIT), count)]
        rows = pl.ds(pl.multiple_of(me * count, UNIT), count)
        return (qo_ref if index == 3 else go_ref).at[rows, :]

    def head_copy(index, step):
        owner = lax.rem(me + step, head_devices)
        return pltpu.make_async_remote_copy(
            src_ref=source(index, owner), dst_ref=target(index),
            send_sem=head_send.at[index, step - 1], recv_sem=head_recv.at[index, step - 1],
            device_id={"head": owner}, device_id_type=MESH,
        )

    def own_copy(index):
        return pltpu.make_async_copy(source(index, me), target(index), own_sem.at[index])

    wide = xo_ref.shape[2]
    own_group = block * pairs + side

    def group_copy(step):
        peer = group_list[step - 1]
        at = peer["blk"] * pairs + peer["dp"]
        return pltpu.make_async_remote_copy(
            src_ref=x_ref.at[:, pl.ds(pl.multiple_of(at * wide, HD), wide)],
            dst_ref=xo_ref.at[own_group],
            send_sem=group_send.at[step - 1], recv_sem=group_recv.at[step - 1],
            device_id=peer, device_id_type=MESH,
        )

    own_x = pltpu.make_async_copy(
        x_ref.at[:, pl.ds(pl.multiple_of(own_group * wide, HD), wide)],
        xo_ref.at[own_group], own_sem.at[5],
    )
    head_steps = range(1, head_devices)
    group_steps = range(1, blocks * pairs)
    for index in (0, 1, 2):
        own_copy(index).start()
        for step in head_steps:
            head_copy(index, step).start()
    for index in (3, 4):
        for step in head_steps:
            head_copy(index, step).start()
        own_copy(index).start()
    for index in (0, 1):
        own_copy(index).wait()
        for step in head_steps:
            head_copy(index, step).wait()

    def shift_copy(which, number):
        shift, first, rows = parts[number]
        at = sum(part[2] for part in parts[number + 1 :])
        ref = (ko_ref, vo_ref)[which]
        return pltpu.make_async_remote_copy(
            src_ref=ref.at[pl.ds(BACK + first, rows), :], dst_ref=ref.at[pl.ds(at, rows), :],
            send_sem=shift_send.at[which, number], recv_sem=shift_recv.at[which, number],
            device_id={"blk": block + shift}, device_id_type=MESH,
        )

    for number, (shift, first, rows) in enumerate(parts):
        at = sum(part[2] for part in parts[number + 1 :])

        @pl.when(block + shift < blocks)
        def _():
            for which in range(2):
                shift_copy(which, number).start()

        @pl.when(block < shift)
        def _():
            for ref in (ko_ref, vo_ref):
                ref[pl.ds(at, rows), :] = jnp.zeros((rows, HD), jnp.bfloat16)

    own_x.start()
    for step in group_steps:
        group_copy(step).start()
    for index in (2, 3, 4):
        own_copy(index).wait()
        for step in head_steps:
            head_copy(index, step).wait()
    for number, (shift, first, rows) in enumerate(parts):

        @pl.when(block + shift < blocks)
        def _():
            for which in range(2):
                shift_copy(which, number).wait_send()

        @pl.when(block >= shift)
        def _():
            for which in range(2):
                shift_copy(which, number).wait_recv()

    own_x.wait()
    for step in group_steps:
        group_copy(step).wait()


def exchange(sizes, parts, queries, grads, keys, values, delta, inputs):
    head_devices, blocks, pairs = sizes
    count = queries.shape[0]
    rows = count * head_devices
    groups = blocks * pairs
    anywhere = pl.BlockSpec(memory_space=pl.ANY)
    inside = pl.BlockSpec(memory_space=pltpu.VMEM)
    dma = pltpu.SemaphoreType.DMA
    wide = queries.shape[1] // head_devices
    return pl.pallas_call(
        functools.partial(exchange_kernel, sizes, parts),
        in_specs=[anywhere, anywhere, inside, inside, inside, anywhere],
        out_specs=[anywhere, anywhere, inside, inside, inside, anywhere],
        out_shape=[
            jax.ShapeDtypeStruct((rows, wide), jnp.bfloat16),
            jax.ShapeDtypeStruct((rows, wide), jnp.bfloat16),
            jax.ShapeDtypeStruct((BACK + rows, HD), jnp.bfloat16),
            jax.ShapeDtypeStruct((BACK + rows, HD), jnp.bfloat16),
            jax.ShapeDtypeStruct((delta.shape[0] // head_devices, rows), jnp.float32),
            jax.ShapeDtypeStruct((groups, count, inputs.shape[1] // groups), jnp.bfloat16),
        ],
        scratch_shapes=[
            dma((5, head_devices - 1)), dma((5, head_devices - 1)), dma((6,)),
            dma((2, len(parts))), dma((2, len(parts))), dma((groups - 1,)), dma((groups - 1,)),
        ],
        compiler_params=pltpu.CompilerParams(
            collective_id=0, has_side_effects=True, vmem_limit_bytes=32 * 1024 * 1024
        ),
    )(queries, grads, keys, values, delta, inputs)


def undo_rotary(grad, cosine, sine):
    half = grad.shape[1] // 2
    first = grad[:, :half]
    second = grad[:, half:]
    return jnp.concatenate([first * cosine + second * sine, second * cosine - first * sine], axis=1)


def window_parts(row_count):
    parts = []
    shift = 1
    left = BACK
    while left > 0:
        count = min(left, row_count)
        parts.append((shift, row_count - count, count))
        left -= count
        shift += 1
    return parts


def swap_heads(array):
    return lax.all_to_all(array, "head", split_axis=1, concat_axis=0, tiled=True)


def on_device(
    layer_input, rot_queries, rot_keys, value_rows, attn_output, output_grad, log_norm, lengths
):
    head_count = log_norm.shape[1]
    head_devices = lax.axis_size("head")
    blocks = lax.axis_size("blk")
    local_count = rot_queries.shape[0]
    row_count = local_count * head_devices
    own_delta = jnp.sum(
        (output_grad.astype(jnp.float32) * attn_output.astype(jnp.float32)).reshape(
            local_count, HQ, HD
        ),
        axis=2,
    )
    parts = window_parts(row_count)
    pairs = lax.axis_size("dp")
    groups = blocks * pairs
    by_kernel = layer_input.shape[1] % (groups * HD) == 0 and pairs == 2
    if by_kernel:
        queries, grads_out, keys, values, delta, inputs = exchange(
            (head_devices, blocks, pairs), parts, rot_queries, output_grad, rot_keys, value_rows,
            own_delta.T, layer_input,
        )
    else:
        queries = swap_heads(rot_queries)
        grads_out = swap_heads(output_grad)
        delta = swap_heads(own_delta).T
        both = swap_heads(
            jnp.concatenate(
                [
                    rot_keys.reshape(local_count, head_devices, -1),
                    value_rows.reshape(local_count, head_devices, -1),
                ],
                axis=2,
            ).reshape(local_count, -1)
        )
        pieces = [both]
        for shift, first, count in parts:
            part = both[first : first + count]
            if shift < blocks:
                part = lax.ppermute(part, "blk", [(b, b + shift) for b in range(blocks - shift)])
            else:
                part = jnp.zeros_like(part)
            pieces.insert(0, part)
        keys_values = jnp.concatenate(pieces, axis=0)
        keys = keys_values[:, :HD]
        values = keys_values[:, HD:]
        inputs = lax.all_to_all(layer_input, ("blk", "dp"), split_axis=1, concat_axis=0, tiled=True)
        inputs = inputs.reshape(groups, local_count, -1)

    lengths_row = lengths[0]
    ends = jnp.cumsum(lengths_row)
    first_row = lax.axis_index("blk") * row_count
    first, position = doc_place(
        ends, lengths_row, first_row + jnp.arange(row_count, dtype=jnp.int32)
    )
    start = (first - first_row + BACK)[None, :]
    steps_j = jnp.arange(HD // 2).astype(jnp.float32)
    inverse = jnp.exp(-math.log(500000.0) * 2.0 * steps_j / HD)
    angle = position.astype(jnp.float32)[:, None] * inverse[None, :]
    cosine = jnp.cos(angle) * SCALE
    sine = jnp.sin(angle) * SCALE

    zero = jnp.zeros((keys.shape[0], HD), jnp.float32)
    shared = (
        queries, grads_out, keys, values, keys.T, (log_norm.T * LOG2E)[:, None, :],
        delta[:, None, :], start, cosine.T, sine.T,
    )
    half = head_count // 2
    dq_first, dk_part, dv_part = attention(0, half, 704, *shared, zero, zero)
    all_first = lax.all_gather(dq_first, ("blk", "dp"), axis=0, tiled=True)
    dq_second, dk_part, dv_part = attention(half, half, 704, *shared, dk_part, dv_part)
    all_second = lax.all_gather(dq_second, ("blk", "dp"), axis=0, tiled=True)

    inputs = lax.all_gather(inputs, "head", axis=1, tiled=True).reshape(groups * row_count, -1)
    key_sums = jnp.concatenate([dk_part, dv_part], axis=1)
    total = key_sums[BACK:]
    at = BACK
    for shift, first, count in parts:
        at -= count
        if shift < blocks:
            got = lax.ppermute(
                key_sums[at : at + count].astype(jnp.bfloat16),
                "blk",
                [(b + shift, b) for b in range(blocks - shift)],
            ).astype(jnp.float32)
            total = total + jnp.pad(got, ((first, 0), (0, 0)))
    key_grads = jnp.concatenate(
        [undo_rotary(total[:, :HD], cosine, sine), total[:, HD:]], axis=1
    ).astype(jnp.bfloat16)
    all_keys = lax.all_gather(key_grads, ("blk", "dp"), axis=0, tiled=True)

    dw_first = contract_rows(inputs, all_first)
    dw_second = contract_rows(inputs, all_second)
    dw_keys = contract_rows(inputs, all_keys)
    return (
        jnp.concatenate([dw_first, dw_second], axis=1),
        dw_keys[:, :HD],
        dw_keys[:, HD:],
    )


def solution(mesh):
    placed = (
        P(("dp", "blk", "head"), None),
        P(("dp", "blk", "head"), None),
        P(("dp", "blk", "head"), None),
        P(("dp", "blk", "head"), None),
        P(("dp", "blk", "head"), None),
        P(("dp", "blk", "head"), None),
        P(("dp", "blk"), "head"),
        P("dp", None),
    )
    return jax.shard_map(
        on_device,
        mesh=mesh,
        in_specs=placed,
        out_specs=(P(("blk", "dp"), "head"), P(("blk", "dp"), "head"), P(("blk", "dp"), "head")),
        check_vma=False,
    )
```

```python
import functools
import math

import jax
import jax.numpy as jnp
from jax import lax
from jax.experimental import pallas as pl
from jax.experimental.pallas import tpu as pltpu
from jax.sharding import PartitionSpec as P

HQ = 32
HD = 128
GQ = 8
UNIT = 128
MOST_LEN = 1280
BACK = MOST_LEN - UNIT
TILE = 256
LOG2E = math.log2(math.e)
SCALE = HD ** (-0.5)


def contract_rows(left, right):
    return lax.dot_general(
        left, right, (((0,), (0,)), ((), ())), preferred_element_type=jnp.float32
    )


def contract_cols(left, right):
    return lax.dot_general(
        left, right, (((1,), (1,)), ((), ())), preferred_element_type=jnp.float32
    )


def doc_place(ends, lengths_row, index):
    after = (index[:, None] >= ends[None, :]).astype(jnp.int32)
    first = jnp.sum(after * lengths_row[None, :], axis=1)
    return (first, index - first)


def attention_kernel(
    chunk, q_ref, g_ref, k_ref, v_ref, kt_ref, norm_ref, delta_ref, start_ref, cos_ref, sin_ref,
    dk_in_ref, dv_in_ref, dq_ref, dk_ref, dv_ref, bias_ref
):
    rows = q_ref.shape[0]
    tiles = rows // TILE
    span = TILE + BACK

    @pl.when(pl.program_id(0) == 0)
    def _():
        dk_ref[...] = dk_in_ref[...]
        dv_ref[...] = dv_in_ref[...]
        for j in range(tiles):
            key_at = lax.broadcasted_iota(jnp.int32, (span, TILE), 0) + j * TILE
            query_at = lax.broadcasted_iota(jnp.int32, (span, TILE), 1) + (j * TILE + BACK)
            first = start_ref[:, j * TILE : (j + 1) * TILE]
            allowed = (key_at >= first) & (key_at <= query_at)
            bias_ref[j] = jnp.where(allowed, 0.0, -1e30)

    for j in range(tiles):
        here = slice(j * TILE, (j + 1) * TILE)
        query = q_ref[here, :]
        grad = g_ref[here, :]
        norm = norm_ref[0, :, here]
        delta = delta_ref[0, :, here]
        dq_t = jnp.zeros((HD, TILE), jnp.float32)
        for c in range(0, span, chunk):
            keys = slice(j * TILE + c, j * TILE + c + chunk)
            score = contract_cols(k_ref[keys, :], query)
            prob = jnp.exp2((score * (SCALE * LOG2E) - norm) + bias_ref[j, c : c + chunk, :])
            dprob = contract_cols(v_ref[keys, :], grad)
            dscore = (prob * (dprob - delta)).astype(jnp.bfloat16)
            dv_ref[keys, :] += jnp.dot(
                prob.astype(jnp.bfloat16), grad, preferred_element_type=jnp.float32
            )
            dk_ref[keys, :] += jnp.dot(dscore, query, preferred_element_type=jnp.float32)
            dq_t += jnp.dot(kt_ref[:, keys], dscore, preferred_element_type=jnp.float32)
        cosine = cos_ref[:, here]
        sine = sin_ref[:, here]
        upper = dq_t[: HD // 2]
        lower = dq_t[HD // 2 :]
        turned = jnp.concatenate(
            [upper * cosine + lower * sine, lower * cosine - upper * sine], axis=0
        )
        dq_ref[here, :] = turned.T.astype(jnp.bfloat16)


def attention(first_head, heads, chunk, queries, grads, keys, values, keys_t, norm, delta, start,
              cosine, sine, dk_in, dv_in):
    rows = queries.shape[0]
    window = keys.shape[0]
    whole = lambda shape: pl.BlockSpec(shape, lambda h: (0,) * len(shape))
    per_head = pl.BlockSpec((rows, HD), lambda h: (0, h + first_head))
    per_row = pl.BlockSpec((1, 1, rows), lambda h: (h + first_head, 0, 0))
    work = heads * (rows // TILE) * (TILE + BACK) * TILE
    return pl.pallas_call(
        functools.partial(attention_kernel, chunk),
        grid=(heads,),
        in_specs=[
            per_head, per_head, whole((window, HD)), whole((window, HD)), whole((HD, window)),
            per_row, per_row, whole((1, rows)), whole((HD // 2, rows)), whole((HD // 2, rows)),
            whole((window, HD)), whole((window, HD)),
        ],
        out_specs=[
            pl.BlockSpec((rows, HD), lambda h: (0, h)), whole((window, HD)), whole((window, HD)),
        ],
        out_shape=[
            jax.ShapeDtypeStruct((rows, heads * HD), jnp.bfloat16),
            jax.ShapeDtypeStruct((window, HD), jnp.float32),
            jax.ShapeDtypeStruct((window, HD), jnp.float32),
        ],
        scratch_shapes=[pltpu.VMEM((rows // TILE, TILE + BACK, TILE), jnp.float32)],
        compiler_params=pltpu.CompilerParams(vmem_limit_bytes=40 * 1024 * 1024),
        cost_estimate=pl.CostEstimate(
            flops=work * HD * 10, bytes_accessed=4 * rows * heads * HD, transcendentals=work
        ),
    )(queries, grads, keys, values, keys_t, norm, delta, start, cosine, sine, dk_in, dv_in)


MESH = pl.DeviceIdType.MESH


def greet(peers):
    barrier = pltpu.get_barrier_semaphore()
    for peer in peers:
        pl.semaphore_signal(barrier, inc=1, device_id=peer, device_id_type=MESH)
    pl.semaphore_wait(barrier, len(peers))


def ring_peers(axis, size):
    here = lax.axis_index(axis)
    return [{axis: lax.rem(here + step, size)} for step in range(1, size)]


def group_peers(blocks, pairs):
    block = lax.axis_index("blk")
    side = lax.axis_index("dp")
    peers = []
    for step in range(1, blocks * pairs):
        peers.append(
            {
                "blk": lax.rem(block + step // pairs, blocks),
                "dp": lax.rem(side + step % pairs, pairs),
            }
        )
    return peers


def exchange_kernel(
    sizes, parts, q_ref, g_ref, k_ref, v_ref, d_ref, x_ref,
    qo_ref, go_ref, ko_ref, vo_ref, do_ref, xo_ref,
    head_send, head_recv, own_sem, shift_send, shift_recv, group_send, group_recv,
):
    head_devices, blocks, pairs = sizes
    me = lax.axis_index("head")
    block = lax.axis_index("blk")
    side = lax.axis_index("dp")
    count = q_ref.shape[0]
    head_list = ring_peers("head", head_devices)
    group_list = group_peers(blocks, pairs)
    greet(head_list + group_list)

    def source(index, owner):
        if index == 0:
            return k_ref.at[:, pl.ds(pl.multiple_of(owner * HD, HD), HD)]
        if index == 1:
            return v_ref.at[:, pl.ds(pl.multiple_of(owner * HD, HD), HD)]
        if index == 2:
            rows = d_ref.shape[0] // head_devices
            return d_ref.at[pl.ds(pl.multiple_of(owner * rows, 8), rows), :]
        wide = q_ref.shape[1] // head_devices
        columns = pl.ds(pl.multiple_of(owner * wide, HD), wide)
        return (q_ref if index == 3 else g_ref).at[:, columns]

    def target(index):
        if index <= 1:
            rows = pl.ds(pl.multiple_of(BACK + me * count, UNIT), count)
            return (ko_ref if index == 0 else vo_ref).at[rows, :]
        if index == 2:
            return do_ref.at[:, pl.ds(pl.multiple_of(me * count, UNIT), count)]
        rows = pl.ds(pl.multiple_of(me * count, UNIT), count)
        return (qo_ref if index == 3 else go_ref).at[rows, :]

    def head_copy(index, step):
        owner = lax.rem(me + step, head_devices)
        return pltpu.make_async_remote_copy(
            src_ref=source(index, owner), dst_ref=target(index),
            send_sem=head_send.at[index, step - 1], recv_sem=head_recv.at[index, step - 1],
            device_id={"head": owner}, device_id_type=MESH,
        )

    def own_copy(index):
        return pltpu.make_async_copy(source(index, me), target(index), own_sem.at[index])

    wide = xo_ref.shape[2]
    own_group = block * pairs + side

    def group_copy(step):
        peer = group_list[step - 1]
        at = peer["blk"] * pairs + peer["dp"]
        return pltpu.make_async_remote_copy(
            src_ref=x_ref.at[:, pl.ds(pl.multiple_of(at * wide, HD), wide)],
            dst_ref=xo_ref.at[own_group],
            send_sem=group_send.at[step - 1], recv_sem=group_recv.at[step - 1],
            device_id=peer, device_id_type=MESH,
        )

    own_x = pltpu.make_async_copy(
        x_ref.at[:, pl.ds(pl.multiple_of(own_group * wide, HD), wide)],
        xo_ref.at[own_group], own_sem.at[5],
    )
    head_steps = range(1, head_devices)
    group_steps = range(1, blocks * pairs)
    for index in (0, 1, 2):
        own_copy(index).start()
        for step in head_steps:
            head_copy(index, step).start()
    for index in (3, 4):
        for step in head_steps:
            head_copy(index, step).start()
        own_copy(index).start()
    for index in (0, 1):
        own_copy(index).wait()
        for step in head_steps:
            head_copy(index, step).wait()

    def shift_copy(which, number):
        shift, first, rows = parts[number]
        at = sum(part[2] for part in parts[number + 1 :])
        ref = (ko_ref, vo_ref)[which]
        return pltpu.make_async_remote_copy(
            src_ref=ref.at[pl.ds(BACK + first, rows), :], dst_ref=ref.at[pl.ds(at, rows), :],
            send_sem=shift_send.at[which, number], recv_sem=shift_recv.at[which, number],
            device_id={"blk": block + shift}, device_id_type=MESH,
        )

    for number, (shift, first, rows) in enumerate(parts):
        at = sum(part[2] for part in parts[number + 1 :])

        @pl.when(block + shift < blocks)
        def _():
            for which in range(2):
                shift_copy(which, number).start()

        @pl.when(block < shift)
        def _():
            for ref in (ko_ref, vo_ref):
                ref[pl.ds(at, rows), :] = jnp.zeros((rows, HD), jnp.bfloat16)

    own_x.start()
    for step in group_steps:
        group_copy(step).start()
    for index in (2, 3, 4):
        own_copy(index).wait()
        for step in head_steps:
            head_copy(index, step).wait()
    for number, (shift, first, rows) in enumerate(parts):

        @pl.when(block + shift < blocks)
        def _():
            for which in range(2):
                shift_copy(which, number).wait_send()

        @pl.when(block >= shift)
        def _():
            for which in range(2):
                shift_copy(which, number).wait_recv()

    own_x.wait()
    for step in group_steps:
        group_copy(step).wait()


def exchange(sizes, parts, queries, grads, keys, values, delta, inputs):
    head_devices, blocks, pairs = sizes
    count = queries.shape[0]
    rows = count * head_devices
    groups = blocks * pairs
    anywhere = pl.BlockSpec(memory_space=pl.ANY)
    inside = pl.BlockSpec(memory_space=pltpu.VMEM)
    dma = pltpu.SemaphoreType.DMA
    wide = queries.shape[1] // head_devices
    return pl.pallas_call(
        functools.partial(exchange_kernel, sizes, parts),
        in_specs=[anywhere, anywhere, inside, inside, inside, anywhere],
        out_specs=[anywhere, anywhere, inside, inside, inside, anywhere],
        out_shape=[
            jax.ShapeDtypeStruct((rows, wide), jnp.bfloat16),
            jax.ShapeDtypeStruct((rows, wide), jnp.bfloat16),
            jax.ShapeDtypeStruct((BACK + rows, HD), jnp.bfloat16),
            jax.ShapeDtypeStruct((BACK + rows, HD), jnp.bfloat16),
            jax.ShapeDtypeStruct((delta.shape[0] // head_devices, rows), jnp.float32),
            jax.ShapeDtypeStruct((groups, count, inputs.shape[1] // groups), jnp.bfloat16),
        ],
        scratch_shapes=[
            dma((5, head_devices - 1)), dma((5, head_devices - 1)), dma((6,)),
            dma((2, len(parts))), dma((2, len(parts))), dma((groups - 1,)), dma((groups - 1,)),
        ],
        compiler_params=pltpu.CompilerParams(
            collective_id=0, has_side_effects=True, vmem_limit_bytes=32 * 1024 * 1024
        ),
    )(queries, grads, keys, values, delta, inputs)


def gather_kernel(
    sizes, parts, dq_ref, kp_ref, ko_ref, cos_ref, sin_ref, x_ref,
    dwq_ref, dwk_ref, dwv_ref,
    land, got, inputs, turned, total, keys_sum,
    key_send, key_recv, x_send, x_recv, own_sem, up_send, up_recv, down_send, down_recv,
    side_send, side_recv,
):
    head_devices, blocks, pairs = sizes
    me = lax.axis_index("head")
    block = lax.axis_index("blk")
    side = lax.axis_index("dp")
    other = 1 - side
    rows = dq_ref.shape[0]
    count = rows // head_devices
    wide = 2 * HD
    chunks = land.shape[1]
    head_list = ring_peers("head", head_devices)
    greet(head_list + ring_peers("blk", blocks) + [{"dp": other}])

    def key_copy(number):
        shift, first, size = parts[number]
        at = sum(part[2] for part in parts[number + 1 :])
        return pltpu.make_async_remote_copy(
            src_ref=kp_ref.at[pl.ds(at, size), :], dst_ref=got.at[pl.ds(at, size), :],
            send_sem=key_send.at[number], recv_sem=key_recv.at[number],
            device_id={"blk": block - shift}, device_id_type=MESH,
        )

    def chain_copy(hop, owner, chunk, up):
        spot = land.at[owner * pairs + side, chunk]
        return pltpu.make_async_remote_copy(
            src_ref=spot, dst_ref=spot,
            send_sem=(up_send if up else down_send).at[hop, chunk],
            recv_sem=(up_recv if up else down_recv).at[hop, chunk],
            device_id={"blk": block + 1 if up else block - 1}, device_id_type=MESH,
        )

    def side_copy(owner, chunk, from_side):
        spot = land.at[owner * pairs + from_side, chunk]
        return pltpu.make_async_remote_copy(
            src_ref=spot, dst_ref=spot, send_sem=side_send.at[owner, chunk],
            recv_sem=side_recv.at[owner, chunk], device_id={"dp": other}, device_id_type=MESH,
        )

    def x_copy(step):
        mine = pl.ds(pl.multiple_of(me * count, UNIT), count)
        return pltpu.make_async_remote_copy(
            src_ref=x_ref, dst_ref=inputs.at[:, mine, :], send_sem=x_send.at[step - 1],
            recv_sem=x_recv.at[step - 1], device_id=head_list[step - 1], device_id_type=MESH,
        )

    def push(owner, hop, chunk):
        @pl.when((block + 1 < blocks) & (owner <= block))
        def _():
            chain_copy(hop, owner, chunk, True).start()

        @pl.when((block >= 1) & (owner >= block))
        def _():
            chain_copy(hop, owner, chunk, False).start()

        side_copy(owner, chunk, side).start()

    for number, (shift, first, size) in enumerate(parts):
        at = sum(part[2] for part in parts[number + 1 :])

        @pl.when(block >= shift)
        def _():
            key_copy(number).start()

        @pl.when(block + shift >= blocks)
        def _():
            got[pl.ds(at, size), :] = jnp.zeros((size, wide), jnp.bfloat16)

    own_group = block * pairs + side
    for chunk in range(chunks - 1):
        land[own_group, chunk] = dq_ref[:, chunk * wide : (chunk + 1) * wide]
        push(block, 0, chunk)
    own_x = pltpu.make_async_copy(
        x_ref, inputs.at[:, pl.ds(pl.multiple_of(me * count, UNIT), count), :], own_sem.at[0]
    )
    own_x.start()
    for step in range(1, head_devices):
        x_copy(step).start()
    keys_sum[...] = ko_ref[...]
    for number, (shift, first, size) in enumerate(parts):
        at = sum(part[2] for part in parts[number + 1 :])

        @pl.when(block + shift < blocks)
        def _():
            key_copy(number).wait_recv()

        keys_sum[first : first + size, :] += got[pl.ds(at, size), :].astype(jnp.float32)

    dk = keys_sum[:, :HD]
    dk = dk * cos_ref[...] + pltpu.roll(dk, HD // 2, 1) * sin_ref[...]
    land[own_group, chunks - 1, :, :HD] = dk.astype(jnp.bfloat16)
    land[own_group, chunks - 1, :, HD:] = keys_sum[:, HD:].astype(jnp.bfloat16)
    push(block, 0, chunks - 1)

    own_x.wait()
    for step in range(1, head_devices):
        x_copy(step).wait_recv()
    total[...] = jnp.zeros_like(total)

    def multiply(group):
        turned[...] = inputs[group].T

        @pl.loop(0, chunks)
        def _(chunk):
            total[chunk] += jnp.dot(
                turned[...], land[group, chunk], preferred_element_type=jnp.float32
            )

    def take(owner, hop, up):
        @pl.loop(0, chunks)
        def _(chunk):
            chain_copy(hop, owner, chunk, up).wait_recv()

            @pl.when((block + 1 < blocks) if up else (block >= 1))
            def _():
                chain_copy(hop + 1, owner, chunk, up).start()

            side_copy(owner, chunk, side).start()

    def finish(owner):
        multiply(owner * pairs + side)

        @pl.loop(0, chunks)
        def _(chunk):
            side_copy(owner, chunk, other).wait_recv()

        multiply(owner * pairs + other)

    finish(block)
    for hop in range(blocks - 1):
        below = block - 1 - hop
        above = block + 1 + hop

        @pl.when(below >= 0)
        def _():
            take(below, hop, True)

        @pl.when(above < blocks)
        def _():
            take(above, hop, False)

        @pl.when(below >= 0)
        def _():
            finish(below)

        @pl.when(above < blocks)
        def _():
            finish(above)

    for chunk in range(chunks - 1):
        dwq_ref[:, chunk * wide : (chunk + 1) * wide] = total[chunk]
    dwk_ref[...] = total[chunks - 1, :, :HD]
    dwv_ref[...] = total[chunks - 1, :, HD:]

    for number, (shift, first, size) in enumerate(parts):

        @pl.when(block >= shift)
        def _():
            key_copy(number).wait_send()

    for step in range(1, head_devices):
        x_copy(step).wait_send()

    @pl.loop(0, chunks)
    def _(chunk):
        for owner in range(blocks):
            side_copy(owner, chunk, side).wait_send()
        for hop in range(blocks - 1):

            @pl.when((block + 1 < blocks) & (block >= hop))
            def _():
                chain_copy(hop, block - hop, chunk, True).wait_send()

            @pl.when((block >= 1) & (block + hop < blocks))
            def _():
                chain_copy(hop, block + hop, chunk, False).wait_send()


def gather_multiply(sizes, parts, dq, key_parts, own_keys, cosine, sine, inputs):
    head_devices, blocks, pairs = sizes
    rows = dq.shape[0]
    groups, count, features = inputs.shape
    chunks = dq.shape[1] // (2 * HD) + 1
    inside = pl.BlockSpec(memory_space=pltpu.VMEM)
    dma = pltpu.SemaphoreType.DMA
    return pl.pallas_call(
        functools.partial(gather_kernel, sizes, parts),
        in_specs=[inside] * 6,
        out_specs=[inside] * 3,
        out_shape=[
            jax.ShapeDtypeStruct((features, dq.shape[1]), jnp.float32),
            jax.ShapeDtypeStruct((features, HD), jnp.float32),
            jax.ShapeDtypeStruct((features, HD), jnp.float32),
        ],
        scratch_shapes=[
            pltpu.VMEM((groups, chunks, rows, 2 * HD), jnp.bfloat16),
            pltpu.VMEM(key_parts.shape, jnp.bfloat16),
            pltpu.VMEM((groups, rows, features), jnp.bfloat16),
            pltpu.VMEM((features, rows), jnp.bfloat16),
            pltpu.VMEM((chunks, features, 2 * HD), jnp.float32),
            pltpu.VMEM(own_keys.shape, jnp.float32),
            dma((len(parts),)), dma((len(parts),)),
            dma((head_devices - 1,)), dma((head_devices - 1,)), dma((1,)),
            dma((blocks, chunks)), dma((blocks, chunks)),
            dma((blocks, chunks)), dma((blocks, chunks)),
            dma((blocks, chunks)), dma((blocks, chunks)),
        ],
        compiler_params=pltpu.CompilerParams(
            collective_id=1, has_side_effects=True, vmem_limit_bytes=48 * 1024 * 1024
        ),
    )(dq, key_parts, own_keys, cosine, sine, inputs)


def undo_rotary(grad, cosine, sine):
    half = grad.shape[1] // 2
    first = grad[:, :half]
    second = grad[:, half:]
    return jnp.concatenate([first * cosine + second * sine, second * cosine - first * sine], axis=1)


def window_parts(row_count):
    parts = []
    shift = 1
    left = BACK
    while left > 0:
        count = min(left, row_count)
        parts.append((shift, row_count - count, count))
        left -= count
        shift += 1
    return parts


def swap_heads(array):
    return lax.all_to_all(array, "head", split_axis=1, concat_axis=0, tiled=True)


def on_device(
    layer_input, rot_queries, rot_keys, value_rows, attn_output, output_grad, log_norm, lengths
):
    head_count = log_norm.shape[1]
    head_devices = lax.axis_size("head")
    blocks = lax.axis_size("blk")
    local_count = rot_queries.shape[0]
    row_count = local_count * head_devices
    own_delta = jnp.sum(
        (output_grad.astype(jnp.float32) * attn_output.astype(jnp.float32)).reshape(
            local_count, HQ, HD
        ),
        axis=2,
    )
    parts = window_parts(row_count)
    pairs = lax.axis_size("dp")
    groups = blocks * pairs
    by_kernel = layer_input.shape[1] % (groups * HD) == 0 and pairs == 2
    if by_kernel:
        queries, grads_out, keys, values, delta, inputs = exchange(
            (head_devices, blocks, pairs), parts, rot_queries, output_grad, rot_keys, value_rows,
            own_delta.T, layer_input,
        )
    else:
        queries = swap_heads(rot_queries)
        grads_out = swap_heads(output_grad)
        delta = swap_heads(own_delta).T
        both = swap_heads(
            jnp.concatenate(
                [
                    rot_keys.reshape(local_count, head_devices, -1),
                    value_rows.reshape(local_count, head_devices, -1),
                ],
                axis=2,
            ).reshape(local_count, -1)
        )
        pieces = [both]
        for shift, first, count in parts:
            part = both[first : first + count]
            if shift < blocks:
                part = lax.ppermute(part, "blk", [(b, b + shift) for b in range(blocks - shift)])
            else:
                part = jnp.zeros_like(part)
            pieces.insert(0, part)
        keys_values = jnp.concatenate(pieces, axis=0)
        keys = keys_values[:, :HD]
        values = keys_values[:, HD:]
        inputs = lax.all_to_all(layer_input, ("blk", "dp"), split_axis=1, concat_axis=0, tiled=True)
        inputs = inputs.reshape(groups, local_count, -1)

    lengths_row = lengths[0]
    ends = jnp.cumsum(lengths_row)
    first_row = lax.axis_index("blk") * row_count
    first, position = doc_place(
        ends, lengths_row, first_row + jnp.arange(row_count, dtype=jnp.int32)
    )
    start = (first - first_row + BACK)[None, :]
    steps_j = jnp.arange(HD // 2).astype(jnp.float32)
    inverse = jnp.exp(-math.log(500000.0) * 2.0 * steps_j / HD)
    angle = position.astype(jnp.float32)[:, None] * inverse[None, :]
    cosine = jnp.cos(angle) * SCALE
    sine = jnp.sin(angle) * SCALE

    zero = jnp.zeros((keys.shape[0], HD), jnp.float32)
    shared = (
        queries, grads_out, keys, values, keys.T, (log_norm.T * LOG2E)[:, None, :],
        delta[:, None, :], start, cosine.T, sine.T,
    )
    if by_kernel:
        dq, dk_part, dv_part = attention(0, head_count, 704, *shared, zero, zero)
        key_sums = jnp.concatenate([dk_part, dv_part], axis=1)
        return tuple(
            gather_multiply(
                (head_devices, blocks, pairs), parts, dq, key_sums[:BACK].astype(jnp.bfloat16),
                key_sums[BACK:], jnp.concatenate([cosine, cosine], axis=1),
                jnp.concatenate([sine, -sine], axis=1), inputs,
            )
        )
    half = head_count // 2
    dq_first, dk_part, dv_part = attention(0, half, 704, *shared, zero, zero)
    all_first = lax.all_gather(dq_first, ("blk", "dp"), axis=0, tiled=True)
    dq_second, dk_part, dv_part = attention(half, half, 704, *shared, dk_part, dv_part)
    all_second = lax.all_gather(dq_second, ("blk", "dp"), axis=0, tiled=True)

    inputs = lax.all_gather(inputs, "head", axis=1, tiled=True).reshape(groups * row_count, -1)
    key_sums = jnp.concatenate([dk_part, dv_part], axis=1)
    total = key_sums[BACK:]
    at = BACK
    for shift, first, count in parts:
        at -= count
        if shift < blocks:
            got = lax.ppermute(
                key_sums[at : at + count].astype(jnp.bfloat16),
                "blk",
                [(b + shift, b) for b in range(blocks - shift)],
            ).astype(jnp.float32)
            total = total + jnp.pad(got, ((first, 0), (0, 0)))
    key_grads = jnp.concatenate(
        [undo_rotary(total[:, :HD], cosine, sine), total[:, HD:]], axis=1
    ).astype(jnp.bfloat16)
    all_keys = lax.all_gather(key_grads, ("blk", "dp"), axis=0, tiled=True)

    dw_first = contract_rows(inputs, all_first)
    dw_second = contract_rows(inputs, all_second)
    dw_keys = contract_rows(inputs, all_keys)
    return (
        jnp.concatenate([dw_first, dw_second], axis=1),
        dw_keys[:, :HD],
        dw_keys[:, HD:],
    )


def solution(mesh):
    placed = (
        P(("dp", "blk", "head"), None),
        P(("dp", "blk", "head"), None),
        P(("dp", "blk", "head"), None),
        P(("dp", "blk", "head"), None),
        P(("dp", "blk", "head"), None),
        P(("dp", "blk", "head"), None),
        P(("dp", "blk"), "head"),
        P("dp", None),
    )
    return jax.shard_map(
        on_device,
        mesh=mesh,
        in_specs=placed,
        out_specs=(P(("blk", "dp"), "head"), P(("blk", "dp"), "head"), P(("blk", "dp"), "head")),
        check_vma=False,
    )
```

```python
import functools
import math

import jax
import jax.numpy as jnp
from jax import lax
from jax.experimental import pallas as pl
from jax.experimental.pallas import tpu as pltpu
from jax.sharding import PartitionSpec as P

HQ = 32
HD = 128
GQ = 8
UNIT = 128
MOST_LEN = 1280
BACK = MOST_LEN - UNIT
TILE = 256
LOG2E = math.log2(math.e)
SCALE = HD ** (-0.5)


def contract_rows(left, right):
    return lax.dot_general(
        left, right, (((0,), (0,)), ((), ())), preferred_element_type=jnp.float32
    )


def contract_cols(left, right):
    return lax.dot_general(
        left, right, (((1,), (1,)), ((), ())), preferred_element_type=jnp.float32
    )


def doc_place(ends, lengths_row, index):
    after = (index[:, None] >= ends[None, :]).astype(jnp.int32)
    first = jnp.sum(after * lengths_row[None, :], axis=1)
    return (first, index - first)


def attention_kernel(
    chunk, q_ref, g_ref, k_ref, v_ref, kt_ref, norm_ref, delta_ref, start_ref, cos_ref, sin_ref,
    dk_in_ref, dv_in_ref, dq_ref, dk_ref, dv_ref, bias_ref
):
    rows = q_ref.shape[0]
    tiles = rows // TILE
    span = TILE + BACK

    @pl.when(pl.program_id(0) == 0)
    def _():
        dk_ref[...] = dk_in_ref[...]
        dv_ref[...] = dv_in_ref[...]
        for j in range(tiles):
            key_at = lax.broadcasted_iota(jnp.int32, (span, TILE), 0) + j * TILE
            query_at = lax.broadcasted_iota(jnp.int32, (span, TILE), 1) + (j * TILE + BACK)
            first = start_ref[:, j * TILE : (j + 1) * TILE]
            allowed = (key_at >= first) & (key_at <= query_at)
            bias_ref[j] = jnp.where(allowed, 0.0, -1e30)

    for j in range(tiles):
        here = slice(j * TILE, (j + 1) * TILE)
        query = q_ref[here, :]
        grad = g_ref[here, :]
        norm = norm_ref[0, :, here]
        delta = delta_ref[0, :, here]
        dq_t = jnp.zeros((HD, TILE), jnp.float32)
        for c in range(0, span, chunk):
            keys = slice(j * TILE + c, j * TILE + c + chunk)
            score = contract_cols(k_ref[keys, :], query)
            prob = jnp.exp2((score * (SCALE * LOG2E) - norm) + bias_ref[j, c : c + chunk, :])
            dprob = contract_cols(v_ref[keys, :], grad)
            dscore = (prob * (dprob - delta)).astype(jnp.bfloat16)
            dv_ref[keys, :] += jnp.dot(
                prob.astype(jnp.bfloat16), grad, preferred_element_type=jnp.float32
            )
            dk_ref[keys, :] += jnp.dot(dscore, query, preferred_element_type=jnp.float32)
            dq_t += jnp.dot(kt_ref[:, keys], dscore, preferred_element_type=jnp.float32)
        cosine = cos_ref[:, here]
        sine = sin_ref[:, here]
        upper = dq_t[: HD // 2]
        lower = dq_t[HD // 2 :]
        turned = jnp.concatenate(
            [upper * cosine + lower * sine, lower * cosine - upper * sine], axis=0
        )
        dq_ref[here, :] = turned.T.astype(jnp.bfloat16)


def attention(first_head, heads, chunk, queries, grads, keys, values, keys_t, norm, delta, start,
              cosine, sine, dk_in, dv_in):
    rows = queries.shape[0]
    window = keys.shape[0]
    whole = lambda shape: pl.BlockSpec(shape, lambda h: (0,) * len(shape))
    per_head = pl.BlockSpec((rows, HD), lambda h: (0, h + first_head))
    per_row = pl.BlockSpec((1, 1, rows), lambda h: (h + first_head, 0, 0))
    work = heads * (rows // TILE) * (TILE + BACK) * TILE
    return pl.pallas_call(
        functools.partial(attention_kernel, chunk),
        grid=(heads,),
        in_specs=[
            per_head, per_head, whole((window, HD)), whole((window, HD)), whole((HD, window)),
            per_row, per_row, whole((1, rows)), whole((HD // 2, rows)), whole((HD // 2, rows)),
            whole((window, HD)), whole((window, HD)),
        ],
        out_specs=[
            pl.BlockSpec((rows, HD), lambda h: (0, h)), whole((window, HD)), whole((window, HD)),
        ],
        out_shape=[
            jax.ShapeDtypeStruct((rows, heads * HD), jnp.bfloat16),
            jax.ShapeDtypeStruct((window, HD), jnp.float32),
            jax.ShapeDtypeStruct((window, HD), jnp.float32),
        ],
        scratch_shapes=[pltpu.VMEM((rows // TILE, TILE + BACK, TILE), jnp.float32)],
        compiler_params=pltpu.CompilerParams(vmem_limit_bytes=58 * 1024 * 1024),
        cost_estimate=pl.CostEstimate(
            flops=work * HD * 10, bytes_accessed=4 * rows * heads * HD, transcendentals=work
        ),
    )(queries, grads, keys, values, keys_t, norm, delta, start, cosine, sine, dk_in, dv_in)


MESH = pl.DeviceIdType.MESH


def greet(peers):
    barrier = pltpu.get_barrier_semaphore()
    for peer in peers:
        pl.semaphore_signal(barrier, inc=1, device_id=peer, device_id_type=MESH)
    pl.semaphore_wait(barrier, len(peers))


def ring_peers(axis, size):
    here = lax.axis_index(axis)
    return [{axis: lax.rem(here + step, size)} for step in range(1, size)]


def group_peers(blocks, pairs):
    block = lax.axis_index("blk")
    side = lax.axis_index("dp")
    peers = []
    for step in range(1, blocks * pairs):
        peers.append(
            {
                "blk": lax.rem(block + step // pairs, blocks),
                "dp": lax.rem(side + step % pairs, pairs),
            }
        )
    return peers


def exchange_kernel(
    sizes, parts, q_ref, g_ref, k_ref, v_ref, o_ref, x_ref,
    qo_ref, go_ref, ko_ref, vo_ref, do_ref, xo_ref,
    d_ref, head_send, head_recv, own_sem, shift_send, shift_recv, group_send, group_recv,
):
    head_devices, blocks, pairs = sizes
    me = lax.axis_index("head")
    block = lax.axis_index("blk")
    side = lax.axis_index("dp")
    count = q_ref.shape[0]
    head_list = ring_peers("head", head_devices)
    group_list = group_peers(blocks, pairs)
    greet(head_list + group_list)

    def source(index, owner):
        if index == 0:
            return k_ref.at[:, pl.ds(pl.multiple_of(owner * HD, HD), HD)]
        if index == 1:
            return v_ref.at[:, pl.ds(pl.multiple_of(owner * HD, HD), HD)]
        if index == 2:
            rows = d_ref.shape[0] // head_devices
            return d_ref.at[pl.ds(pl.multiple_of(owner * rows, 8), rows), :]
        wide = q_ref.shape[1] // head_devices
        columns = pl.ds(pl.multiple_of(owner * wide, HD), wide)
        return (q_ref if index == 3 else g_ref).at[:, columns]

    def target(index):
        if index <= 1:
            rows = pl.ds(pl.multiple_of(BACK + me * count, UNIT), count)
            return (ko_ref if index == 0 else vo_ref).at[rows, :]
        if index == 2:
            return do_ref.at[:, pl.ds(pl.multiple_of(me * count, UNIT), count)]
        rows = pl.ds(pl.multiple_of(me * count, UNIT), count)
        return (qo_ref if index == 3 else go_ref).at[rows, :]

    def head_copy(index, step):
        owner = lax.rem(me + step, head_devices)
        return pltpu.make_async_remote_copy(
            src_ref=source(index, owner), dst_ref=target(index),
            send_sem=head_send.at[index, step - 1], recv_sem=head_recv.at[index, step - 1],
            device_id={"head": owner}, device_id_type=MESH,
        )

    def own_copy(index):
        return pltpu.make_async_copy(source(index, me), target(index), own_sem.at[index])

    wide = xo_ref.shape[2]
    own_group = block * pairs + side

    def group_copy(step):
        peer = group_list[step - 1]
        at = peer["blk"] * pairs + peer["dp"]
        return pltpu.make_async_remote_copy(
            src_ref=x_ref.at[:, pl.ds(pl.multiple_of(at * wide, HD), wide)],
            dst_ref=xo_ref.at[own_group],
            send_sem=group_send.at[step - 1], recv_sem=group_recv.at[step - 1],
            device_id=peer, device_id_type=MESH,
        )

    own_x = pltpu.make_async_copy(
        x_ref.at[:, pl.ds(pl.multiple_of(own_group * wide, HD), wide)],
        xo_ref.at[own_group], own_sem.at[5],
    )
    head_steps = range(1, head_devices)
    group_steps = range(1, blocks * pairs)
    for index in (0, 1):
        own_copy(index).start()
        for step in head_steps:
            head_copy(index, step).start()
    own_x.start()
    for step in group_steps:
        group_copy(step).start()
    for index in (3, 4):
        for step in head_steps:
            head_copy(index, step).start()
        own_copy(index).start()
    for index in (0, 1):
        own_copy(index).wait()
        for step in head_steps:
            head_copy(index, step).wait()

    def shift_copy(which, number):
        shift, first, rows = parts[number]
        at = sum(part[2] for part in parts[number + 1 :])
        ref = (ko_ref, vo_ref)[which]
        return pltpu.make_async_remote_copy(
            src_ref=ref.at[pl.ds(BACK + first, rows), :], dst_ref=ref.at[pl.ds(at, rows), :],
            send_sem=shift_send.at[which, number], recv_sem=shift_recv.at[which, number],
            device_id={"blk": block + shift}, device_id_type=MESH,
        )

    for number, (shift, first, rows) in enumerate(parts):
        at = sum(part[2] for part in parts[number + 1 :])

        @pl.when(block + shift < blocks)
        def _():
            for which in range(2):
                shift_copy(which, number).start()

        @pl.when(block < shift)
        def _():
            for ref in (ko_ref, vo_ref):
                ref[pl.ds(at, rows), :] = jnp.zeros((rows, HD), jnp.bfloat16)

    for head in range(d_ref.shape[0]):
        columns = slice(head * HD, (head + 1) * HD)
        product = g_ref[:, columns].astype(jnp.float32) * o_ref[:, columns].astype(jnp.float32)
        d_ref[head : head + 1, :] = jnp.sum(product.T, axis=0, keepdims=True)
    own_copy(2).start()
    for step in head_steps:
        head_copy(2, step).start()
    for index in (2, 3, 4):
        own_copy(index).wait()
        for step in head_steps:
            head_copy(index, step).wait()
    for number, (shift, first, rows) in enumerate(parts):

        @pl.when(block + shift < blocks)
        def _():
            for which in range(2):
                shift_copy(which, number).wait_send()

        @pl.when(block >= shift)
        def _():
            for which in range(2):
                shift_copy(which, number).wait_recv()

    own_x.wait()
    for step in group_steps:
        group_copy(step).wait()


def exchange(sizes, parts, queries, grads, keys, values, outputs, inputs):
    head_devices, blocks, pairs = sizes
    count = queries.shape[0]
    rows = count * head_devices
    groups = blocks * pairs
    anywhere = pl.BlockSpec(memory_space=pl.ANY)
    inside = pl.BlockSpec(memory_space=pltpu.VMEM)
    dma = pltpu.SemaphoreType.DMA
    wide = queries.shape[1] // head_devices
    return pl.pallas_call(
        functools.partial(exchange_kernel, sizes, parts),
        in_specs=[anywhere, inside, inside, inside, inside, anywhere],
        out_specs=[anywhere, anywhere, inside, inside, inside, anywhere],
        out_shape=[
            jax.ShapeDtypeStruct((rows, wide), jnp.bfloat16),
            jax.ShapeDtypeStruct((rows, wide), jnp.bfloat16),
            jax.ShapeDtypeStruct((BACK + rows, HD), jnp.bfloat16),
            jax.ShapeDtypeStruct((BACK + rows, HD), jnp.bfloat16),
            jax.ShapeDtypeStruct((HQ // head_devices, rows), jnp.float32),
            jax.ShapeDtypeStruct((groups, count, inputs.shape[1] // groups), jnp.bfloat16),
        ],
        scratch_shapes=[
            pltpu.VMEM((HQ, count), jnp.float32),
            dma((5, head_devices - 1)), dma((5, head_devices - 1)), dma((6,)),
            dma((2, len(parts))), dma((2, len(parts))), dma((groups - 1,)), dma((groups - 1,)),
        ],
        compiler_params=pltpu.CompilerParams(
            collective_id=0, has_side_effects=True, vmem_limit_bytes=32 * 1024 * 1024
        ),
    )(queries, grads, keys, values, outputs, inputs)


def gather_kernel(
    sizes, parts, dq_ref, kp_ref, ko_ref, cos_ref, sin_ref, x_ref,
    dwq_ref, dwk_ref, dwv_ref,
    land, got, inputs, turned, total, keys_sum,
    key_send, key_recv, x_send, x_recv, own_sem, up_send, up_recv, down_send, down_recv,
    side_send, side_recv,
):
    head_devices, blocks, pairs = sizes
    me = lax.axis_index("head")
    block = lax.axis_index("blk")
    side = lax.axis_index("dp")
    other = 1 - side
    rows = dq_ref.shape[0]
    count = rows // head_devices
    wide = 2 * HD
    chunks = land.shape[1]
    head_list = ring_peers("head", head_devices)
    greet(head_list + ring_peers("blk", blocks) + [{"dp": other}])

    def key_copy(number):
        shift, first, size = parts[number]
        at = sum(part[2] for part in parts[number + 1 :])
        return pltpu.make_async_remote_copy(
            src_ref=kp_ref.at[pl.ds(at, size), :], dst_ref=got.at[pl.ds(at, size), :],
            send_sem=key_send.at[number], recv_sem=key_recv.at[number],
            device_id={"blk": block - shift}, device_id_type=MESH,
        )

    def chain_copy(hop, owner, chunk, up):
        spot = land.at[owner * pairs + side, chunk]
        return pltpu.make_async_remote_copy(
            src_ref=spot, dst_ref=spot,
            send_sem=(up_send if up else down_send).at[hop, chunk],
            recv_sem=(up_recv if up else down_recv).at[hop, chunk],
            device_id={"blk": block + 1 if up else block - 1}, device_id_type=MESH,
        )

    def side_copy(owner, chunk, from_side):
        spot = land.at[owner * pairs + from_side, chunk]
        return pltpu.make_async_remote_copy(
            src_ref=spot, dst_ref=spot, send_sem=side_send.at[owner, chunk],
            recv_sem=side_recv.at[owner, chunk], device_id={"dp": other}, device_id_type=MESH,
        )

    def x_copy(step):
        mine = pl.ds(pl.multiple_of(me * count, UNIT), count)
        return pltpu.make_async_remote_copy(
            src_ref=x_ref, dst_ref=inputs.at[:, mine, :], send_sem=x_send.at[step - 1],
            recv_sem=x_recv.at[step - 1], device_id=head_list[step - 1], device_id_type=MESH,
        )

    def push(owner, hop, chunk):
        @pl.when((block + 1 < blocks) & (owner <= block))
        def _():
            chain_copy(hop, owner, chunk, True).start()

        @pl.when((block >= 1) & (owner >= block))
        def _():
            chain_copy(hop, owner, chunk, False).start()

        side_copy(owner, chunk, side).start()

    for number, (shift, first, size) in enumerate(parts):
        at = sum(part[2] for part in parts[number + 1 :])

        @pl.when(block >= shift)
        def _():
            key_copy(number).start()

        @pl.when(block + shift >= blocks)
        def _():
            got[pl.ds(at, size), :] = jnp.zeros((size, wide), jnp.bfloat16)

    own_group = block * pairs + side
    for chunk in range(chunks - 1):
        land[own_group, chunk] = dq_ref[:, chunk * wide : (chunk + 1) * wide]
        push(block, 0, chunk)
    own_x = pltpu.make_async_copy(
        x_ref, inputs.at[:, pl.ds(pl.multiple_of(me * count, UNIT), count), :], own_sem.at[0]
    )
    own_x.start()
    for step in range(1, head_devices):
        x_copy(step).start()
    keys_sum[...] = ko_ref[...]
    for number, (shift, first, size) in enumerate(parts):
        at = sum(part[2] for part in parts[number + 1 :])

        @pl.when(block + shift < blocks)
        def _():
            key_copy(number).wait_recv()

        keys_sum[first : first + size, :] += got[pl.ds(at, size), :].astype(jnp.float32)

    dk = keys_sum[:, :HD]
    dk = dk * cos_ref[...] + pltpu.roll(dk, HD // 2, 1) * sin_ref[...]
    land[own_group, chunks - 1, :, :HD] = dk.astype(jnp.bfloat16)
    land[own_group, chunks - 1, :, HD:] = keys_sum[:, HD:].astype(jnp.bfloat16)
    push(block, 0, chunks - 1)

    own_x.wait()
    for step in range(1, head_devices):
        x_copy(step).wait_recv()
    total[...] = jnp.zeros_like(total)

    def multiply(group):
        turned[...] = inputs[group].T

        @pl.loop(0, chunks)
        def _(chunk):
            total[chunk] += jnp.dot(
                turned[...], land[group, chunk], preferred_element_type=jnp.float32
            )

    def take(owner, hop, up):
        @pl.loop(0, chunks)
        def _(chunk):
            chain_copy(hop, owner, chunk, up).wait_recv()

            @pl.when((block + 1 < blocks) if up else (block >= 1))
            def _():
                chain_copy(hop + 1, owner, chunk, up).start()

            side_copy(owner, chunk, side).start()

    def finish(owner):
        multiply(owner * pairs + side)

        @pl.loop(0, chunks)
        def _(chunk):
            side_copy(owner, chunk, other).wait_recv()

        multiply(owner * pairs + other)

    finish(block)
    for hop in range(blocks - 1):
        below = block - 1 - hop
        above = block + 1 + hop

        @pl.when(below >= 0)
        def _():
            take(below, hop, True)

        @pl.when(above < blocks)
        def _():
            take(above, hop, False)

        @pl.when(below >= 0)
        def _():
            finish(below)

        @pl.when(above < blocks)
        def _():
            finish(above)

    for chunk in range(chunks - 1):
        dwq_ref[:, chunk * wide : (chunk + 1) * wide] = total[chunk]
    dwk_ref[...] = total[chunks - 1, :, :HD]
    dwv_ref[...] = total[chunks - 1, :, HD:]

    for number, (shift, first, size) in enumerate(parts):

        @pl.when(block >= shift)
        def _():
            key_copy(number).wait_send()

    for step in range(1, head_devices):
        x_copy(step).wait_send()

    @pl.loop(0, chunks)
    def _(chunk):
        for owner in range(blocks):
            side_copy(owner, chunk, side).wait_send()
        for hop in range(blocks - 1):

            @pl.when((block + 1 < blocks) & (block >= hop))
            def _():
                chain_copy(hop, block - hop, chunk, True).wait_send()

            @pl.when((block >= 1) & (block + hop < blocks))
            def _():
                chain_copy(hop, block + hop, chunk, False).wait_send()


def gather_multiply(sizes, parts, dq, key_parts, own_keys, cosine, sine, inputs):
    head_devices, blocks, pairs = sizes
    rows = dq.shape[0]
    groups, count, features = inputs.shape
    chunks = dq.shape[1] // (2 * HD) + 1
    inside = pl.BlockSpec(memory_space=pltpu.VMEM)
    dma = pltpu.SemaphoreType.DMA
    return pl.pallas_call(
        functools.partial(gather_kernel, sizes, parts),
        in_specs=[inside] * 6,
        out_specs=[inside] * 3,
        out_shape=[
            jax.ShapeDtypeStruct((features, dq.shape[1]), jnp.float32),
            jax.ShapeDtypeStruct((features, HD), jnp.float32),
            jax.ShapeDtypeStruct((features, HD), jnp.float32),
        ],
        scratch_shapes=[
            pltpu.VMEM((groups, chunks, rows, 2 * HD), jnp.bfloat16),
            pltpu.VMEM(key_parts.shape, jnp.bfloat16),
            pltpu.VMEM((groups, rows, features), jnp.bfloat16),
            pltpu.VMEM((features, rows), jnp.bfloat16),
            pltpu.VMEM((chunks, features, 2 * HD), jnp.float32),
            pltpu.VMEM(own_keys.shape, jnp.float32),
            dma((len(parts),)), dma((len(parts),)),
            dma((head_devices - 1,)), dma((head_devices - 1,)), dma((1,)),
            dma((blocks, chunks)), dma((blocks, chunks)),
            dma((blocks, chunks)), dma((blocks, chunks)),
            dma((blocks, chunks)), dma((blocks, chunks)),
        ],
        compiler_params=pltpu.CompilerParams(
            collective_id=1, has_side_effects=True, vmem_limit_bytes=48 * 1024 * 1024
        ),
    )(dq, key_parts, own_keys, cosine, sine, inputs)


def undo_rotary(grad, cosine, sine):
    half = grad.shape[1] // 2
    first = grad[:, :half]
    second = grad[:, half:]
    return jnp.concatenate([first * cosine + second * sine, second * cosine - first * sine], axis=1)


def window_parts(row_count):
    parts = []
    shift = 1
    left = BACK
    while left > 0:
        count = min(left, row_count)
        parts.append((shift, row_count - count, count))
        left -= count
        shift += 1
    return parts


def swap_heads(array):
    return lax.all_to_all(array, "head", split_axis=1, concat_axis=0, tiled=True)


def on_device(
    layer_input, rot_queries, rot_keys, value_rows, attn_output, output_grad, log_norm, lengths
):
    head_count = log_norm.shape[1]
    head_devices = lax.axis_size("head")
    blocks = lax.axis_size("blk")
    local_count = rot_queries.shape[0]
    row_count = local_count * head_devices
    parts = window_parts(row_count)
    pairs = lax.axis_size("dp")
    groups = blocks * pairs
    by_kernel = layer_input.shape[1] % (groups * HD) == 0 and pairs == 2
    if by_kernel:
        queries, grads_out, keys, values, delta, inputs = exchange(
            (head_devices, blocks, pairs), parts, rot_queries, output_grad, rot_keys, value_rows,
            attn_output, layer_input,
        )
    else:
        queries = swap_heads(rot_queries)
        grads_out = swap_heads(output_grad)
        own_delta = jnp.sum(
            (output_grad.astype(jnp.float32) * attn_output.astype(jnp.float32)).reshape(
                local_count, HQ, HD
            ),
            axis=2,
        )
        delta = swap_heads(own_delta).T
        both = swap_heads(
            jnp.concatenate(
                [
                    rot_keys.reshape(local_count, head_devices, -1),
                    value_rows.reshape(local_count, head_devices, -1),
                ],
                axis=2,
            ).reshape(local_count, -1)
        )
        pieces = [both]
        for shift, first, count in parts:
            part = both[first : first + count]
            if shift < blocks:
                part = lax.ppermute(part, "blk", [(b, b + shift) for b in range(blocks - shift)])
            else:
                part = jnp.zeros_like(part)
            pieces.insert(0, part)
        keys_values = jnp.concatenate(pieces, axis=0)
        keys = keys_values[:, :HD]
        values = keys_values[:, HD:]
        inputs = lax.all_to_all(layer_input, ("blk", "dp"), split_axis=1, concat_axis=0, tiled=True)
        inputs = inputs.reshape(groups, local_count, -1)

    lengths_row = lengths[0]
    ends = jnp.cumsum(lengths_row)
    first_row = lax.axis_index("blk") * row_count
    first, position = doc_place(
        ends, lengths_row, first_row + jnp.arange(row_count, dtype=jnp.int32)
    )
    start = (first - first_row + BACK)[None, :]
    steps_j = jnp.arange(HD // 2).astype(jnp.float32)
    inverse = jnp.exp(-math.log(500000.0) * 2.0 * steps_j / HD)
    angle = position.astype(jnp.float32)[:, None] * inverse[None, :]
    cosine = jnp.cos(angle) * SCALE
    sine = jnp.sin(angle) * SCALE

    zero = jnp.zeros((keys.shape[0], HD), jnp.float32)
    shared = (
        queries, grads_out, keys, values, keys.T, (log_norm.T * LOG2E)[:, None, :],
        delta[:, None, :], start, cosine.T, sine.T,
    )
    if by_kernel:
        dq, dk_part, dv_part = attention(0, head_count, 704, *shared, zero, zero)
        key_sums = jnp.concatenate([dk_part, dv_part], axis=1)
        return tuple(
            gather_multiply(
                (head_devices, blocks, pairs), parts, dq, key_sums[:BACK].astype(jnp.bfloat16),
                key_sums[BACK:], jnp.concatenate([cosine, cosine], axis=1),
                jnp.concatenate([sine, -sine], axis=1), inputs,
            )
        )
    half = head_count // 2
    dq_first, dk_part, dv_part = attention(0, half, 704, *shared, zero, zero)
    all_first = lax.all_gather(dq_first, ("blk", "dp"), axis=0, tiled=True)
    dq_second, dk_part, dv_part = attention(half, half, 704, *shared, dk_part, dv_part)
    all_second = lax.all_gather(dq_second, ("blk", "dp"), axis=0, tiled=True)

    inputs = lax.all_gather(inputs, "head", axis=1, tiled=True).reshape(groups * row_count, -1)
    key_sums = jnp.concatenate([dk_part, dv_part], axis=1)
    total = key_sums[BACK:]
    at = BACK
    for shift, first, count in parts:
        at -= count
        if shift < blocks:
            got = lax.ppermute(
                key_sums[at : at + count].astype(jnp.bfloat16),
                "blk",
                [(b + shift, b) for b in range(blocks - shift)],
            ).astype(jnp.float32)
            total = total + jnp.pad(got, ((first, 0), (0, 0)))
    key_grads = jnp.concatenate(
        [undo_rotary(total[:, :HD], cosine, sine), total[:, HD:]], axis=1
    ).astype(jnp.bfloat16)
    all_keys = lax.all_gather(key_grads, ("blk", "dp"), axis=0, tiled=True)

    dw_first = contract_rows(inputs, all_first)
    dw_second = contract_rows(inputs, all_second)
    dw_keys = contract_rows(inputs, all_keys)
    return (
        jnp.concatenate([dw_first, dw_second], axis=1),
        dw_keys[:, :HD],
        dw_keys[:, HD:],
    )


def solution(mesh):
    placed = (
        P(("dp", "blk", "head"), None),
        P(("dp", "blk", "head"), None),
        P(("dp", "blk", "head"), None),
        P(("dp", "blk", "head"), None),
        P(("dp", "blk", "head"), None),
        P(("dp", "blk", "head"), None),
        P(("dp", "blk"), "head"),
        P("dp", None),
    )
    return jax.shard_map(
        on_device,
        mesh=mesh,
        in_specs=placed,
        out_specs=(P(("blk", "dp"), "head"), P(("blk", "dp"), "head"), P(("blk", "dp"), "head")),
        check_vma=False,
    )
```
